32 devices in a mesh: rep: 16 (over z, y, core), seq: 2 (over x).
Axes of the slice: x: 2, y: 2, z: 4, core: 2. Of those that a mesh axis runs over, the one named last changes fastest.
Arguments:
- text_tokens: bfloat16 [16, 512, 3072], P('rep', 'seq'), may hold values from -6 to 6
- image_tokens: bfloat16 [16, 576, 3072], P('rep', 'seq'), may hold values from -6 to 6
- weights: bfloat16 [2, 3072, 3, 3072], P(None, ('rep', 'seq'))
- qk_gain: float32 [2, 2, 128], replicated, may hold values from 0.5 to 4.2, as said below
- mod_table: float32 [28, 2, 2, 3072], replicated, may hold values from -3 to 3
- text_lengths: int32 [16], P('rep'), may hold values from 64 to 512, as said below
- time_index: int32 [16], P('rep'), may hold values from 0 to 27
Outputs:
- attended_text: bfloat16 [16, 512, 3072], P('rep', 'seq')
- attended_image: bfloat16 [16, 576, 3072], P('rep', 'seq')
The draws below stay inside these ranges and needn't reach their ends.
Inputs may be any that keep to these rules, and one draw needn't show every extreme that they name: `text_lengths`: padding of a prompt lies past its length; some prompt fills all 512 text tokens. `qk_gain`: positive gains.
All inputs are finite; a program needn't handle non-finite values.
Results may differ from the reference program's by a relative error of at most 0.01.
Values may be sent and summed in bfloat16 or wider, within the bound.
No kernel may reach another device: no remote copies, remote signals or barrier semaphores. Data moves between devices by JAX's collectives and lax.ppermute only.
A program may use at most 192 MiB of HBM per device.

```python
import jax
import jax.numpy as jnp
from jax import lax

D = 3072
HEADS = 24
HD = 128
GRID = 24
TXT = 512
STEPS = 28
IMG = 576
REPLICAS = 16


def draw_weights(key, part):
    key = jax.random.fold_in(key, 11)
    base = jax.random.normal(key, (2, D, 3, D), jnp.float32) * D ** (-0.5)
    return base.astype(jnp.bfloat16)


def draw_qk_gain(key, part):
    key = jax.random.fold_in(key, 12)
    return jnp.exp(jax.random.uniform(key, (2, 2, HD), jnp.float32, -0.69, 0.69))


def draw_text_lengths(key, part):
    key = jax.random.fold_in(key, 13)
    first_key, second_key = jax.random.split(key)
    length_draw = jax.random.randint(first_key, (REPLICAS,), TXT // 8, TXT + 1)
    chosen = jax.random.randint(second_key, (), 0, REPLICAS)
    return jnp.where(jnp.arange(REPLICAS) == chosen, TXT, length_draw).astype(jnp.int32)


def touch_ends(array, own_key, low, top_value):
    extent = array.shape
    place = [jax.random.randint(jax.random.fold_in(own_key, axis), (), 0, extent[axis]) for axis in range(len(extent))]
    array = array.at[tuple(place)].set(low)
    longest = extent.index(max(extent))
    place[longest] = (place[longest] + 1) % extent[longest]
    return array.at[tuple(place)].set(top_value)


def shard_levels(own_key, shape, cuts, smallest, largest):
    loudness = 1.0
    for dim, parts in cuts:
        steps = jax.random.uniform(jax.random.fold_in(jax.random.fold_in(own_key, 6), dim), (parts,), jnp.float32, smallest / len(cuts), largest / len(cuts))
        loudness = loudness * jnp.repeat(jnp.exp(steps), shape[dim] // parts).reshape((-1,) + (1,) * (len(shape) - 1 - dim))
    return loudness


def noise(own_key, extent, deviation, most, shards=(), kind=jnp.bfloat16):
    entries = jax.random.normal(own_key, extent, jnp.float32) * deviation
    if len(shards) > 0:
        entries = shard_levels(own_key, extent, shards, -0.22, 0.18) * entries
    return jnp.clip(entries, min=-most, max=most).astype(kind)


def setup_inputs(seed: int = 0) -> dict:
    key_of = jax.random.split(jax.random.key(seed), 8)
    text_tokens = noise(key_of[0], (REPLICAS, TXT, D), 1.0, 6.0, ((0, 16), (1, 2)))
    image_tokens = noise(key_of[1], (REPLICAS, IMG, D), 1.0, 6.0, ((0, 16), (1, 2)))
    weights = draw_weights(jax.random.fold_in(key_of[7], 71), 0)
    qk_gain = draw_qk_gain(jax.random.fold_in(key_of[7], 71), 0)
    mod_table = noise(key_of[4], (STEPS, 2, 2, D), 0.5, 3.0, (), jnp.float32)
    text_lengths = draw_text_lengths(jax.random.fold_in(key_of[7], 71), 0)
    time_index = touch_ends(jax.random.randint(key_of[6], (REPLICAS,), 0, STEPS), jax.random.fold_in(key_of[6], 1), 0, STEPS - 1).astype(jnp.int32)
    return dict(text_tokens=text_tokens, image_tokens=image_tokens, weights=weights, qk_gain=qk_gain, mod_table=mod_table, text_lengths=text_lengths, time_index=time_index)


def layer_modulate(tokens, shift_row, scale_row):
    values = tokens.astype(jnp.float32)
    center = values - lax.optimization_barrier(jnp.mean(values, axis=-1, keepdims=True))
    spread = lax.optimization_barrier(jnp.mean(center * center, axis=-1, keepdims=True))
    normed = center * lax.rsqrt(spread + 1e-06)
    return (normed * (1.0 + shift_row * 0.0 + scale_row) + shift_row).astype(jnp.bfloat16)

def rope_tables(length, text_count, grid_side, head_dim):
    pair_count = head_dim // 2
    still_pairs = head_dim // 16
    row_pairs = (pair_count - still_pairs) // 2
    col_pairs = pair_count - still_pairs - row_pairs
    position = jnp.arange(length, dtype=jnp.int32)
    image_pos = jnp.maximum(position - text_count, 0)
    is_image = (position >= text_count).astype(jnp.float32)
    row_pos = (image_pos // grid_side).astype(jnp.float32) * is_image
    col_pos = (image_pos % grid_side).astype(jnp.float32) * is_image
    row_freq = 10000.0 ** (-jnp.arange(row_pairs, dtype=jnp.float32) / row_pairs)
    col_freq = 10000.0 ** (-jnp.arange(col_pairs, dtype=jnp.float32) / col_pairs)
    angles = jnp.concatenate([jnp.zeros((length, still_pairs), jnp.float32), row_pos[:, None] * row_freq[None, :], col_pos[:, None] * col_freq[None, :]], axis=1)
    return (jnp.cos(angles), jnp.sin(angles))

def rotate(values, cosine, sine):
    shaped = values.reshape(values.shape[0], values.shape[1], -1, 2)
    first_part = shaped[..., 0]
    second_part = shaped[..., 1]
    cos_part = cosine[:, None, :]
    sin_part = sine[:, None, :]
    turned = jnp.stack([first_part * cos_part - second_part * sin_part, first_part * sin_part + second_part * cos_part], axis=-1)
    return turned.reshape(values.shape)

def normalize_heads(values, gain):
    power = lax.optimization_barrier(jnp.mean(values * values, axis=-1, keepdims=True))
    return values * lax.rsqrt(power + 1e-06) * gain

def prepare_heads(projected, gain, cosine, sine):
    query = rotate(normalize_heads(projected[:, 0], gain[0]), cosine, sine).astype(jnp.bfloat16)
    key_part = rotate(normalize_heads(projected[:, 1], gain[1]), cosine, sine).astype(jnp.bfloat16)
    value_part = projected[:, 2].astype(jnp.bfloat16)
    return (query, key_part, value_part)

def attend_head(query_head, key_head, value_head, allowed):
    scores = lax.dot_general(query_head, key_head, (((1,), (1,)), ((), ())), preferred_element_type=jnp.float32)
    scores = scores * query_head.shape[-1] ** (-0.5)
    scores = jnp.where(allowed[None, :], scores, -jnp.inf)
    row_max = lax.optimization_barrier(jnp.max(scores, axis=-1, keepdims=True))
    exponent = jnp.exp(scores - row_max)
    softmax_out = (exponent / lax.optimization_barrier(jnp.sum(exponent, axis=-1, keepdims=True))).astype(jnp.bfloat16)
    return jnp.dot(softmax_out, value_head, preferred_element_type=jnp.float32).astype(jnp.bfloat16)

def run_attention(queries, keys_all, values_all, allowed):

    def one_head(trio):
        return attend_head(trio[0], trio[1], trio[2], allowed)
    stacked = (jnp.moveaxis(queries, 1, 0), jnp.moveaxis(keys_all, 1, 0), jnp.moveaxis(values_all, 1, 0))
    outputs = lax.map(one_head, stacked)
    outputs = jnp.moveaxis(outputs, 0, 1)
    return outputs.reshape(outputs.shape[0], -1)

def reference(text_tokens, image_tokens, weights, qk_gain, mod_table, text_lengths, time_index):
    total_rows = TXT + IMG
    cosine_all, sine_all = rope_tables(total_rows, TXT, GRID, HD)
    position = jnp.arange(total_rows, dtype=jnp.int32)

    def one_sample(operands):
        text_rows, image_rows, live_count, step_index = operands
        table_row = lax.dynamic_index_in_dim(mod_table, step_index, 0, keepdims=False)
        prepared = []
        for stream in range(2):
            rows_here = (text_rows, image_rows)[stream]
            modded = layer_modulate(rows_here, table_row[stream, 0], table_row[stream, 1])
            flat_weight = weights[stream].reshape(D, 3 * D)
            projected = jnp.dot(modded, flat_weight, preferred_element_type=jnp.float32)
            row_count = rows_here.shape[0]
            offset_rows = 0 if stream == 0 else TXT
            projected = projected.reshape(row_count, 3, HEADS, HD)
            prepared.append(prepare_heads(projected, qk_gain[stream], cosine_all[offset_rows:offset_rows + row_count], sine_all[offset_rows:offset_rows + row_count]))
        queries = jnp.concatenate([prepared[0][0], prepared[1][0]], axis=0)
        keys_all = jnp.concatenate([prepared[0][1], prepared[1][1]], axis=0)
        values_all = jnp.concatenate([prepared[0][2], prepared[1][2]], axis=0)
        allowed = (position >= TXT) | (position < live_count)
        joined = run_attention(queries, keys_all, values_all, allowed)
        return (joined[:TXT], joined[TXT:])
    return lax.map(one_sample, (text_tokens, image_tokens, text_lengths.astype(jnp.int32), time_index.astype(jnp.int32)))
```

```python
import functools

import jax
import jax.numpy as jnp
import numpy as np
from jax import lax
from jax.experimental import pallas as pl
from jax.experimental.pallas import tpu as pltpu
from jax.sharding import PartitionSpec as P

D = 3072
HEADS = 24
HD = 128
GRID = 24
TXT = 512
IMG = GRID * GRID
TOTAL = TXT + IMG
CHUNK = 32
KEYS = 9 * HD
ABSENT = -1e30
LOG2E = 1.4426950408889634


def head_groups(heads):
    if heads < 4:
        return [1] * heads
    return [heads - heads // 3, heads // 3]


def rope_image_tables():
    pair_count = HD // 2
    still_pairs = HD // 16
    row_pairs = (pair_count - still_pairs) // 2
    col_pairs = pair_count - still_pairs - row_pairs
    position = np.arange(IMG, dtype=np.int32)
    row_freq = np.float32(10000.0) ** (-np.arange(row_pairs, dtype=np.float32) / np.float32(row_pairs))
    col_freq = np.float32(10000.0) ** (-np.arange(col_pairs, dtype=np.float32) / np.float32(col_pairs))
    angles = np.concatenate(
        [
            np.zeros((IMG, still_pairs), np.float32),
            (position // GRID).astype(np.float32)[:, None] * row_freq[None, :].astype(np.float32),
            (position % GRID).astype(np.float32)[:, None] * col_freq[None, :].astype(np.float32),
        ],
        axis=1,
    ).astype(np.float64)
    cosine = np.repeat(np.cos(angles), 2, axis=1).astype(np.float32)
    sine = np.stack([-np.sin(angles), np.sin(angles)], axis=-1).reshape(IMG, HD).astype(np.float32)
    return cosine, sine


def modulate_kernel(step_index, table, text, image, text_out, image_out):
    for stream, tokens, out in ((0, text, text_out), (1, image, image_out)):
        values = tokens[...].astype(jnp.float32)
        center = values - jnp.mean(values, axis=-1, keepdims=True)
        spread = jnp.mean(center * center, axis=-1, keepdims=True)
        normed = center * lax.rsqrt(spread + 1e-06)
        shift_row = table[0, stream, 0:1, :]
        scale_row = table[0, stream, 1:2, :]
        out[...] = (normed * (1.0 + scale_row) + shift_row).astype(jnp.bfloat16)


def layer_modulate(time_index, mod_table, text, image):
    steps = 4 if text.shape[0] % 64 == 0 and image.shape[0] % 64 == 0 else 1
    steps = 2 if steps == 1 and text.shape[0] % 32 == 0 and image.shape[0] % 32 == 0 else steps
    rows = lambda x: pl.BlockSpec((x.shape[0] // steps, D), lambda i, step_index: (i, 0))
    return pl.pallas_call(
        modulate_kernel,
        grid_spec=pltpu.PrefetchScalarGridSpec(
            num_scalar_prefetch=1,
            grid=(steps,),
            in_specs=[
                pl.BlockSpec((1, 2, 2, D), lambda i, step_index: (step_index[0], 0, 0, 0)),
                rows(text),
                rows(image),
            ],
            out_specs=[rows(text), rows(image)],
        ),
        out_shape=[jax.ShapeDtypeStruct(x.shape, jnp.bfloat16) for x in (text, image)],
        compiler_params=pltpu.CompilerParams(vmem_limit_bytes=32 * 1024 * 1024),
    )(time_index, mod_table, text, image)


def swap_pairs(values):
    even = lax.broadcasted_iota(jnp.int32, values.shape, 1) % 2 == 0
    return jnp.where(even, pltpu.roll(values, HD - 1, 1), pltpu.roll(values, 1, 1))


def cut_kernel(groups, count, pair, columns, w, *rest):
    outs, sem = rest[:-1], rest[-1]
    copies = []
    for g, (first, heads) in enumerate(groups):
        for t in range(count):
            for h in range(heads):
                begin = pl.multiple_of(columns[t] + (first + h) * HD, HD)
                for s in range(2):
                    for part in range(3):
                        place = ((h // pair * 2 + s) * pair + h % pair) * 3 + part
                        copies.append(
                            pltpu.make_async_copy(
                                w.at[s, part, :, pl.ds(begin, HD)],
                                outs[g * count + t].at[:, pl.ds(place * HD, HD)],
                                sem.at[len(copies)],
                            )
                        )
    for copy in copies:
        copy.start()
    for copy in copies:
        copy.wait()


def cut_pieces(weights, columns, groups, pair):
    count = columns.shape[0]
    rows = weights.shape[2]
    outs = pl.pallas_call(
        functools.partial(cut_kernel, groups, count, pair),
        in_specs=[
            pl.BlockSpec(memory_space=pltpu.SMEM),
            pl.BlockSpec(memory_space=pltpu.HBM),
        ],
        out_specs=[pl.BlockSpec(memory_space=pltpu.VMEM)] * (len(groups) * count),
        out_shape=[
            jax.ShapeDtypeStruct((rows, 6 * heads * HD), jnp.bfloat16)
            for _, heads in groups
            for _ in range(count)
        ],
        scratch_shapes=[
            pltpu.SemaphoreType.DMA((6 * count * sum(heads for _, heads in groups),))
        ],
        compiler_params=pltpu.CompilerParams(vmem_limit_bytes=32 * 1024 * 1024),
    )(columns, weights)
    return [outs[g * count : (g + 1) * count] for g in range(len(groups))]


def stack_kernel(places, *rest):
    for i, piece in enumerate(rest[:-1]):
        rest[-1][places[i]] = piece[...]


def stack_pieces(pieces, places):
    in_vmem = pl.BlockSpec(memory_space=pltpu.VMEM)
    return pl.pallas_call(
        stack_kernel,
        in_specs=[pl.BlockSpec(memory_space=pltpu.SMEM)] + [in_vmem] * len(pieces),
        out_specs=in_vmem,
        out_shape=jax.ShapeDtypeStruct((len(pieces),) + pieces[0].shape, jnp.bfloat16),
        compiler_params=pltpu.CompilerParams(vmem_limit_bytes=32 * 1024 * 1024),
    )(places, *pieces)


def place_kernel(count, columns, *rest):
    pieces, sem = rest[:count], rest[-1]
    text, image = rest[-3], rest[-2]
    copies = []
    for i, piece in enumerate(pieces):
        width = piece.shape[1]
        begin = pl.multiple_of(columns[i], HD)
        start = 0
        for out in (text, image):
            rows = out.shape[0]
            copies.append(
                pltpu.make_async_copy(
                    piece.at[pl.ds(start, rows)],
                    out.at[:, pl.ds(begin, width)],
                    sem.at[len(copies)],
                )
            )
            start += rows
    for copy in copies:
        copy.start()
    for copy in copies:
        copy.wait()


def place_pieces(pieces, columns, outs, text_rows, image_rows):
    count = len(pieces)
    anywhere = pl.BlockSpec(memory_space=pl.ANY)
    return pl.pallas_call(
        functools.partial(place_kernel, count),
        in_specs=[pl.BlockSpec(memory_space=pltpu.SMEM)]
        + [pl.BlockSpec(memory_space=pltpu.VMEM)] * count
        + [anywhere] * len(outs),
        out_specs=[anywhere] * 2,
        out_shape=[
            jax.ShapeDtypeStruct((text_rows, D), jnp.bfloat16),
            jax.ShapeDtypeStruct((image_rows, D), jnp.bfloat16),
        ],
        scratch_shapes=[pltpu.SemaphoreType.DMA((2 * count,))],
        input_output_aliases={1 + count + i: i for i in range(len(outs))},
    )(columns, *pieces, *outs)


def project_stream(x, w, begin, samples, pair, gain, tables, q, k, v, flat):
    rows = x.shape[0] // samples
    flat[...] = jnp.dot(x[...], w, preferred_element_type=jnp.float32)
    for i in range(samples):
        for start in range(0, rows, CHUNK):
            mine = pl.ds(i * rows + start, CHUNK)
            here = pl.ds(begin + start, CHUNK)
            for h in range(pair):
                item = i * pair + h
                for part, target in ((0, q), (1, k)):
                    column = (h * 3 + part) * HD
                    values = flat[mine, column : column + HD]
                    power = jnp.mean(values * values, axis=-1, keepdims=True)
                    if begin == 0:
                        turned = values * gain[part : part + 1, :]
                    else:
                        angle = pl.ds(start, CHUNK)
                        a, b = tables[2 * part], tables[2 * part + 1]
                        turned = values * a[angle, :] + swap_pairs(values) * b[angle, :]
                    turned = turned * lax.rsqrt(power + 1e-06)
                    target[item, here, :HD] = turned.astype(jnp.bfloat16)
                column = (h * 3 + 2) * HD
                v[item, here, :HD] = flat[mine, column : column + HD].astype(jnp.bfloat16)


def attend_block(q, k, v, start, rows, write, score, prob, top):
    score[pl.ds(0, rows), :] = lax.dot_general(
        q[pl.ds(start, rows), :],
        k[...],
        (((1,), (1,)), ((), ())),
        preferred_element_type=jnp.float32,
    )
    for r in range(0, rows, CHUNK):
        row_max = jnp.max(score[pl.ds(r, CHUNK), :], axis=-1, keepdims=True)
        top[pl.ds(r, CHUNK), :] = jnp.broadcast_to(row_max, (CHUNK, HD))
    for r in range(0, rows, CHUNK):
        row_max = top[pl.ds(r, CHUNK), :]
        for tile in range(0, KEYS, HD):
            value = score[pl.ds(r, CHUNK), tile : tile + HD] - row_max
            prob[pl.ds(r, CHUNK), tile : tile + HD] = jnp.exp2(
                value * (HD ** (-0.5) * LOG2E)
            ).astype(jnp.bfloat16)
    mixed = jnp.dot(prob[pl.ds(0, rows), :], v[...], preferred_element_type=jnp.float32)
    write(start, rows, (mixed[:, :HD] / mixed[:, HD:]).astype(jnp.bfloat16))


def group_kernel(
    first, heads, which, pair, apart, rows_from, xt_far, xi_far, w, w_own,
    gain, aq, bq, ak, bk, mask, *rest
):
    samples = len(which)
    steps = heads // pair
    items = samples * pair
    count = samples * 2 if apart else samples
    outs = rest[:count]
    xt, xi, buffers, q_s, k_s, v_s, flat_t, flat_i, scores, probs, tops, sems = rest[count:]
    tables = (aq, bq, ak, bk)
    slots = min(steps, 2)
    width = pair * 3 * HD

    def fetch(h, slot, stream):
        begin = pl.multiple_of((h * 2 + stream) * width, width)
        target = buffers.at[slot, stream]
        if rows_from is None:
            return [
                pltpu.make_async_copy(
                    w.at[:, pl.ds(begin, width)], target, sems.at[2 + slot * 2 + stream]
                )
            ]
        count = rows_from.shape[0]
        copies = []
        for n in range(count):
            if n == 0:
                begin_own = pl.multiple_of(
                    ((first // pair + h) * 2 + stream) * width, width
                )
                part = w_own.at[:, :, :, pl.ds(begin_own, width)]
            else:
                part = w.at[:, :, n - 1, :, pl.ds(begin, width)]
            copies.append(
                pltpu.make_async_copy(
                    part,
                    target.at[:, rows_from[n, 0], :, rows_from[n, 1], :, :],
                    sems.at[2 + (slot * 2 + stream) * count + n],
                )
            )
        return copies

    def start(copies):
        for copy in copies:
            copy.start()

    def wait(copies):
        for copy in copies:
            copy.wait()

    tokens = [
        pltpu.make_async_copy(far.at[pl.ds(which[0] * rows, samples * rows)], near, sems.at[n])
        for n, (far, near, rows) in enumerate(((xt_far, xt, TXT), (xi_far, xi, IMG)))
    ]
    for stream in range(2):
        start(fetch(0, 0, stream))
        tokens[stream].start()
    lead = lax.broadcasted_iota(jnp.int32, (KEYS, HD), 1) == 0
    for slot in range(slots):
        for i in range(items):
            q_s[slot, i, :, HD:] = jnp.where(lead, 1.0, 0.0).astype(jnp.bfloat16)
            k_s[slot, i, :, HD:] = mask[which[i // pair]]
            k_s[slot, i, TOTAL:, :HD] = jnp.zeros((KEYS - TOTAL, HD), jnp.bfloat16)
            v_s[slot, i, :, HD:] = jnp.ones((KEYS, HD), jnp.bfloat16)
            v_s[slot, i, TOTAL:, :HD] = jnp.zeros((KEYS - TOTAL, HD), jnp.bfloat16)

    def project(h, stream):
        slot = h % 2
        project_stream(
            (xt, xi)[stream],
            buffers[slot, stream].reshape(D, width),
            0 if stream == 0 else TXT,
            samples,
            pair,
            gain,
            tables,
            q_s.at[slot],
            k_s.at[slot],
            v_s.at[slot],
            (flat_t, flat_i)[stream],
        )

    def attend(h, i):
        slot = h % 2

        def write(start, rows, block):
            column = (h * pair + i % pair) * HD
            column = column if isinstance(h, int) else pl.multiple_of(column, HD)
            if apart:
                begin = 0 if start < TXT else TXT // 2
                for k in range(2):
                    half = block[k * rows // 2 : (k + 1) * rows // 2]
                    outs[2 * (i // pair) + k][pl.ds(begin, rows // 2), pl.ds(column, HD)] = half
            else:
                outs[i // pair][pl.ds(start, rows), pl.ds(column, HD)] = block

        for n, (start, rows) in enumerate(((0, TXT), (TXT, IMG))):
            attend_block(
                q_s.at[slot, i],
                k_s.at[slot, i],
                v_s.at[slot, i],
                start,
                rows,
                write,
                scores.at[n],
                probs.at[n],
                tops.at[n],
            )

    for stream in range(2):
        wait(fetch(0, 0, stream))
        tokens[stream].wait()
        if steps > 1:
            start(fetch(1, 1, stream))
        project(0, stream)

    def step(h, carry):
        for stream in range(2):
            wait(fetch(h, h % 2, stream))

        @pl.when(h + 1 < steps)
        def _():
            for stream in range(2):
                start(fetch(h + 1, (h + 1) % 2, stream))

        half = max(items // 2, 1)
        project(h, 0)
        for i in range(half):
            attend(h - 1, i)
        project(h, 1)
        for i in range(half, items):
            attend(h - 1, i)
        return carry

    if steps > 1:
        lax.fori_loop(1, steps, step, 0)
    for i in range(items):
        attend(steps - 1, i)


def attend_group(xt, xi, gathered, own, rows_from, tables, mask, first, heads, which, pair, apart):
    samples = len(which)
    count = samples * 2 if apart else samples
    rows = TOTAL // 2 if apart else TOTAL
    slots = min(heads // pair, 2)
    in_vmem = pl.BlockSpec(memory_space=pltpu.VMEM)
    in_hbm = pl.BlockSpec(memory_space=pltpu.HBM)
    kernel = functools.partial(group_kernel, first, heads, which, pair, apart)
    if own is None:
        weight_args, weight_specs, buffer, quarters = [gathered], [in_hbm], (D,), 1
        body = lambda xt, xi, w, *rest: kernel(None, xt, xi, w, None, *rest)
    else:
        outers, cores, _, weight_rows, _ = gathered.shape
        quarters = rows_from.shape[0]
        ranks = quarters // 2
        weight_args = [gathered, own, rows_from]
        weight_specs = [in_hbm, in_hbm, pl.BlockSpec(memory_space=pltpu.SMEM)]
        buffer = (outers, 2, cores, ranks, weight_rows)
        body = lambda xt, xi, w, w_own, places, *rest: kernel(places, xt, xi, w, w_own, *rest)
    return pl.pallas_call(
        body,
        in_specs=[in_hbm] * 2 + weight_specs + [in_vmem] * (len(tables) + 1),
        out_specs=[in_vmem] * count,
        out_shape=[jax.ShapeDtypeStruct((rows, heads * HD), jnp.bfloat16)] * count,
        scratch_shapes=[
            pltpu.VMEM((samples * TXT, D), jnp.bfloat16),
            pltpu.VMEM((samples * IMG, D), jnp.bfloat16),
            pltpu.VMEM((slots, 2) + buffer + (pair * 3 * HD,), jnp.bfloat16),
        ]
        + [pltpu.VMEM((slots, samples * pair, KEYS, 2 * HD), jnp.bfloat16)] * 3
        + [
            pltpu.VMEM((samples * TXT, pair * 3 * HD), jnp.float32),
            pltpu.VMEM((samples * IMG, pair * 3 * HD), jnp.float32),
            pltpu.VMEM((2, IMG, KEYS), jnp.float32),
            pltpu.VMEM((2, IMG, KEYS), jnp.bfloat16),
            pltpu.VMEM((2, IMG, HD), jnp.float32),
            pltpu.SemaphoreType.DMA((2 + 2 * slots * quarters,)),
        ],
        compiler_params=pltpu.CompilerParams(vmem_limit_bytes=56 * 1024 * 1024),
        cost_estimate=pl.CostEstimate(
            flops=samples * heads * (2 * TOTAL * D * 3 * HD + 8 * TOTAL * TOTAL * HD),
            bytes_accessed=heads * D * 6 * HD * 2 + 2 * samples * TOTAL * D,
            transcendentals=samples * heads * TOTAL * TOTAL,
        ),
    )(xt, xi, *weight_args, *tables, mask)


def on_device(text_tokens, image_tokens, weights, qk_gain, mod_table, text_lengths, time_index):
    ranks = lax.axis_size("seq")
    reps = lax.axis_size("rep")
    split = 2 if (HEADS // ranks) % 2 == 0 and reps % 4 == 0 else 1
    cores = 2
    outers = reps // (split * cores)
    rank = lax.axis_index("seq")
    rep = lax.axis_index("rep")
    core = lax.rem(rep, cores)
    f_here = lax.rem(rep // cores, split)
    heads_here = HEADS // (split * ranks)
    cols = heads_here * HD
    weight_rows = weights.shape[1]
    text_rows = text_tokens.shape[1]
    image_rows = image_tokens.shape[1]
    weights = weights.transpose(0, 2, 1, 3)

    def permute(value, target):
        pairs = []
        for o in range(outers):
            for f in range(split):
                for c in range(cores):
                    for r in range(ranks):
                        tf, tc, tr = target(f, c, r)
                        pairs.append(
                            (
                                ((o * split + f) * cores + c) * ranks + r,
                                ((o * split + tf) * cores + tc) * ranks + tr % ranks,
                            )
                        )
        return lax.ppermute(value, ("rep", "seq"), pairs)

    def shift(value, flip, k):
        if flip == 0 and k % ranks == 0:
            return value
        return permute(value, lambda f, c, r: (f ^ flip, c, r + k))

    def source(k):
        return lax.rem(rank - k + ranks, ranks)

    def head_owner(flip, k):
        f = f_here ^ flip if split > 1 else 0
        return f * ranks + lax.rem(rank + k, ranks)

    groups = []
    first = 0
    for heads in head_groups(heads_here):
        groups.append((first, heads))
        first += heads
    pair = 2 if all(first % 2 == 0 and heads % 2 == 0 for first, heads in groups) else 1
    hops = [(a, k) for a in range(split) for k in range(ranks)]
    targets = jnp.stack([head_owner(a, k) * cols for a, k in hops]).astype(jnp.int32)
    places = jnp.stack([source(k) for _, k in hops]).astype(jnp.int32)
    rows_from = None
    if split > 1:
        rows_from = jnp.stack(
            [jnp.stack([f_here ^ a, source(k)]) for a, k in hops]
        ).astype(jnp.int32)
        own_columns = cut_pieces(weights, targets[:1], [(0, heads_here)], pair)[0][0]
        targets, own_columns = lax.optimization_barrier((targets[1:], own_columns))
        hops = hops[1:]
        places = jnp.arange(len(hops), dtype=jnp.int32)
    blocks = []
    for pieces in cut_pieces(weights, targets, groups, pair):
        pieces = [shift(piece, a, k) for piece, (a, k) in zip(pieces, hops)]
        block = stack_pieces(pieces, places)
        blocks.append(block.reshape(len(hops) * weight_rows, block.shape[-1]))

    gather_groups = [
        [(o * split + f) * cores + c for o in range(outers) for c in range(cores)]
        for f in range(split)
    ]

    def gather(block):
        return lax.all_gather(
            block,
            "rep",
            axis=0,
            tiled=True,
            axis_index_groups=gather_groups if split > 1 else None,
        )

    own_weight = gather(own_columns) if split > 1 else None
    modded = layer_modulate(time_index, mod_table, text_tokens[0], image_tokens[0])
    modded, blocks = lax.optimization_barrier((modded, blocks))
    own = [[shift(m, 0, k) for k in range(ranks)] for m in modded]
    other_image = shift(modded[1], 1, 0) if split > 1 else modded[1]
    texts, images = own
    if split > 1:
        texts = texts + [shift(piece, 1, 0) for piece in own[0]]
        images = images + [shift(other_image, 0, k) for k in range(ranks)]
    texts, images = [jnp.concatenate(pieces, axis=0) for pieces in (texts, images)]

    apart = ranks == 2
    order = [source(k) for k in range(ranks)]
    cosine_np, sine_np = rope_image_tables()

    def reorder(table):
        table = jnp.asarray(table)
        return jnp.concatenate(
            [lax.dynamic_slice_in_dim(table, r * image_rows, image_rows, 0) for r in order], axis=0
        )

    cosine, sine = reorder(cosine_np), reorder(sine_np)
    swapped = qk_gain.reshape(2, 2, HD // 2, 2)[..., ::-1].reshape(2, 2, HD)
    tables = [qk_gain[0]]
    for part in range(2):
        tables += [cosine * qk_gain[1, part], sine * swapped[1, part]]
    within = jnp.arange(text_rows, dtype=jnp.int32)
    masks = []
    for flip in range(split):
        live = shift(text_lengths, flip, 0)[0]
        column = [
            jnp.where(r * text_rows + within < live, 0.0, ABSENT).astype(jnp.float32)
            for r in order
        ]
        column.append(jnp.zeros((IMG,), jnp.float32))
        column.append(jnp.full((KEYS - TOTAL,), ABSENT, jnp.float32))
        masks.append(jnp.concatenate(column))
    mask = jnp.where(jnp.arange(HD) == 0, jnp.stack(masks)[:, :, None], 0.0).astype(jnp.bfloat16)

    blocks[-1], texts, images, tables, mask = lax.optimization_barrier(
        (blocks[-1], texts, images, tables, mask)
    )

    def attend(weight, first, heads):
        if split > 1:
            weight = weight.reshape(outers, cores, len(hops), weight_rows, weight.shape[-1])
        received, columns = [], []
        for flip in reversed(range(split)):
            parts = attend_group(
                texts, images, weight, own_quarter, rows_from, tables, mask,
                first, heads, (flip,), pair, apart,
            )
            weight, parts = lax.optimization_barrier((weight, parts))
            if not apart:
                whole = parts[0]
                parts = []
                for k in range(ranks):
                    text = whole[k * text_rows : (k + 1) * text_rows]
                    image = whole[TXT + k * image_rows : TXT + (k + 1) * image_rows]
                    parts.append(jnp.concatenate([text, image], axis=0))
            for k in range(ranks):
                received.append(shift(parts[k], flip, ranks - k))
                columns.append(head_owner(flip, k) * cols + first * HD)
        return received, columns

    def place(received, columns, outs):
        columns = jnp.stack(columns).astype(jnp.int32)
        return place_pieces(received, columns, outs, text_rows, image_rows)

    outs = []
    if split > 1:
        blocks[0], own_weight = lax.optimization_barrier((blocks[0], own_weight))
    weight = gather(blocks[0])
    own_quarter = None
    if split > 1:
        own_quarter = own_weight.reshape(outers, cores, weight_rows, own_weight.shape[-1])
    for g, (first, heads) in enumerate(groups):
        if g + 1 < len(groups):
            block, weight = lax.optimization_barrier((blocks[g + 1], weight))
            following = gather(block)
        outs = place(*attend(weight, first, heads), outs)
        weight = following
    return (outs[0][None], outs[1][None])


def solution(mesh):
    placed = (
        P("rep", "seq", None),
        P("rep", "seq", None),
        P(None, ("rep", "seq"), None, None),
        P(),
        P(),
        P("rep"),
        P("rep"),
    )
    return jax.shard_map(
        on_device,
        mesh=mesh,
        in_specs=placed,
        out_specs=(P("rep", "seq", None), P("rep", "seq", None)),
        check_vma=False,
    )
```

```python
import functools

import jax
import jax.numpy as jnp
import numpy as np
from jax import lax
from jax.experimental import pallas as pl
from jax.experimental.pallas import tpu as pltpu
from jax.sharding import PartitionSpec as P

D = 3072
HEADS = 24
HD = 128
GRID = 24
TXT = 512
IMG = GRID * GRID
TOTAL = TXT + IMG
CHUNK = 32
KEYS = 9 * HD
ABSENT = -1e30
LOG2E = 1.4426950408889634


def head_groups(heads):
    if heads < 4:
        return [1] * heads
    return [heads - heads // 3, heads // 3]


def rope_image_tables():
    pair_count = HD // 2
    still_pairs = HD // 16
    row_pairs = (pair_count - still_pairs) // 2
    col_pairs = pair_count - still_pairs - row_pairs
    position = np.arange(IMG, dtype=np.int32)
    row_freq = np.float32(10000.0) ** (-np.arange(row_pairs, dtype=np.float32) / np.float32(row_pairs))
    col_freq = np.float32(10000.0) ** (-np.arange(col_pairs, dtype=np.float32) / np.float32(col_pairs))
    angles = np.concatenate(
        [
            np.zeros((IMG, still_pairs), np.float32),
            (position // GRID).astype(np.float32)[:, None] * row_freq[None, :].astype(np.float32),
            (position % GRID).astype(np.float32)[:, None] * col_freq[None, :].astype(np.float32),
        ],
        axis=1,
    ).astype(np.float64)
    cosine = np.repeat(np.cos(angles), 2, axis=1).astype(np.float32)
    sine = np.stack([-np.sin(angles), np.sin(angles)], axis=-1).reshape(IMG, HD).astype(np.float32)
    return cosine, sine


def modulate_kernel(step_index, table, text, image, text_out, image_out):
    for stream, tokens, out in ((0, text, text_out), (1, image, image_out)):
        values = tokens[...].astype(jnp.float32)
        center = values - jnp.mean(values, axis=-1, keepdims=True)
        spread = jnp.mean(center * center, axis=-1, keepdims=True)
        normed = center * lax.rsqrt(spread + 1e-06)
        shift_row = table[0, stream, 0:1, :]
        scale_row = table[0, stream, 1:2, :]
        out[...] = (normed * (1.0 + scale_row) + shift_row).astype(jnp.bfloat16)


def layer_modulate(time_index, mod_table, text, image):
    steps = 4 if text.shape[0] % 64 == 0 and image.shape[0] % 64 == 0 else 1
    steps = 2 if steps == 1 and text.shape[0] % 32 == 0 and image.shape[0] % 32 == 0 else steps
    rows = lambda x: pl.BlockSpec((x.shape[0] // steps, D), lambda i, step_index: (i, 0))
    return pl.pallas_call(
        modulate_kernel,
        grid_spec=pltpu.PrefetchScalarGridSpec(
            num_scalar_prefetch=1,
            grid=(steps,),
            in_specs=[
                pl.BlockSpec((1, 2, 2, D), lambda i, step_index: (step_index[0], 0, 0, 0)),
                rows(text),
                rows(image),
            ],
            out_specs=[rows(text), rows(image)],
        ),
        out_shape=[jax.ShapeDtypeStruct(x.shape, jnp.bfloat16) for x in (text, image)],
        compiler_params=pltpu.CompilerParams(vmem_limit_bytes=32 * 1024 * 1024),
    )(time_index, mod_table, text, image)


def swap_pairs(values):
    even = lax.broadcasted_iota(jnp.int32, values.shape, 1) % 2 == 0
    return jnp.where(even, pltpu.roll(values, HD - 1, 1), pltpu.roll(values, 1, 1))


def cut_kernel(groups, count, pair, columns, w, *rest):
    outs, sem = rest[:-1], rest[-1]
    copies = []
    for g, (first, heads) in enumerate(groups):
        for t in range(count):
            for h in range(heads):
                begin = pl.multiple_of(columns[t] + (first + h) * HD, HD)
                for s in range(2):
                    for part in range(3):
                        place = ((h // pair * 2 + s) * pair + h % pair) * 3 + part
                        copies.append(
                            pltpu.make_async_copy(
                                w.at[s, part, :, pl.ds(begin, HD)],
                                outs[g * count + t].at[:, pl.ds(place * HD, HD)],
                                sem.at[len(copies)],
                            )
                        )
    for copy in copies:
        copy.start()
    for copy in copies:
        copy.wait()


def cut_pieces(weights, columns, groups, pair):
    count = columns.shape[0]
    rows = weights.shape[2]
    outs = pl.pallas_call(
        functools.partial(cut_kernel, groups, count, pair),
        in_specs=[
            pl.BlockSpec(memory_space=pltpu.SMEM),
            pl.BlockSpec(memory_space=pltpu.HBM),
        ],
        out_specs=[pl.BlockSpec(memory_space=pltpu.VMEM)] * (len(groups) * count),
        out_shape=[
            jax.ShapeDtypeStruct((rows, 6 * heads * HD), jnp.bfloat16)
            for _, heads in groups
            for _ in range(count)
        ],
        scratch_shapes=[
            pltpu.SemaphoreType.DMA((6 * count * sum(heads for _, heads in groups),))
        ],
        compiler_params=pltpu.CompilerParams(vmem_limit_bytes=58 * 1024 * 1024),
    )(columns, weights)
    return [outs[g * count : (g + 1) * count] for g in range(len(groups))]


def stack_kernel(places, *rest):
    for i, piece in enumerate(rest[:-1]):
        rest[-1][places[i]] = piece[...]


def stack_pieces(pieces, places):
    in_vmem = pl.BlockSpec(memory_space=pltpu.VMEM)
    return pl.pallas_call(
        stack_kernel,
        in_specs=[pl.BlockSpec(memory_space=pltpu.SMEM)] + [in_vmem] * len(pieces),
        out_specs=in_vmem,
        out_shape=jax.ShapeDtypeStruct((len(pieces),) + pieces[0].shape, jnp.bfloat16),
        compiler_params=pltpu.CompilerParams(vmem_limit_bytes=32 * 1024 * 1024),
    )(places, *pieces)


def place_kernel(count, columns, *rest):
    pieces, sem = rest[:count], rest[-1]
    text, image = rest[-3], rest[-2]
    copies = []
    for i, piece in enumerate(pieces):
        width = piece.shape[1]
        begin = pl.multiple_of(columns[i], HD)
        start = 0
        for out in (text, image):
            rows = out.shape[0]
            copies.append(
                pltpu.make_async_copy(
                    piece.at[pl.ds(start, rows)],
                    out.at[:, pl.ds(begin, width)],
                    sem.at[len(copies)],
                )
            )
            start += rows
    for copy in copies:
        copy.start()
    for copy in copies:
        copy.wait()


def place_pieces(pieces, columns, outs, text_rows, image_rows):
    count = len(pieces)
    anywhere = pl.BlockSpec(memory_space=pl.ANY)
    return pl.pallas_call(
        functools.partial(place_kernel, count),
        in_specs=[pl.BlockSpec(memory_space=pltpu.SMEM)]
        + [pl.BlockSpec(memory_space=pltpu.VMEM)] * count
        + [anywhere] * len(outs),
        out_specs=[anywhere] * 2,
        out_shape=[
            jax.ShapeDtypeStruct((text_rows, D), jnp.bfloat16),
            jax.ShapeDtypeStruct((image_rows, D), jnp.bfloat16),
        ],
        scratch_shapes=[pltpu.SemaphoreType.DMA((2 * count,))],
        input_output_aliases={1 + count + i: i for i in range(len(outs))},
    )(columns, *pieces, *outs)


def project_stream(x, w, begin, samples, pair, gain, tables, q, k, v, flat):
    rows = x.shape[0] // samples
    flat[...] = jnp.dot(x[...], w, preferred_element_type=jnp.float32)
    for i in range(samples):
        for start in range(0, rows, CHUNK):
            mine = pl.ds(i * rows + start, CHUNK)
            here = pl.ds(begin + start, CHUNK)
            for h in range(pair):
                item = i * pair + h
                for part, target in ((0, q), (1, k)):
                    column = (h * 3 + part) * HD
                    values = flat[mine, column : column + HD]
                    power = jnp.mean(values * values, axis=-1, keepdims=True)
                    if begin == 0:
                        turned = values * gain[part : part + 1, :]
                    else:
                        angle = pl.ds(start, CHUNK)
                        a, b = tables[2 * part], tables[2 * part + 1]
                        turned = values * a[angle, :] + swap_pairs(values) * b[angle, :]
                    turned = turned * lax.rsqrt(power + 1e-06)
                    target[item, here, :HD] = turned.astype(jnp.bfloat16)
                column = (h * 3 + 2) * HD
                v[item, here, :HD] = flat[mine, column : column + HD].astype(jnp.bfloat16)


def attend_block(q, k, v, start, rows, write, score, prob, top):
    score[pl.ds(0, rows), :] = lax.dot_general(
        q[pl.ds(start, rows), :],
        k[...],
        (((1,), (1,)), ((), ())),
        preferred_element_type=jnp.float32,
    )
    for r in range(0, rows, CHUNK):
        row_max = jnp.max(score[pl.ds(r, CHUNK), :], axis=-1, keepdims=True)
        top[pl.ds(r, CHUNK), :] = jnp.broadcast_to(row_max, (CHUNK, HD))
    for r in range(0, rows, CHUNK):
        row_max = top[pl.ds(r, CHUNK), :]
        for tile in range(0, KEYS, HD):
            value = score[pl.ds(r, CHUNK), tile : tile + HD] - row_max
            prob[pl.ds(r, CHUNK), tile : tile + HD] = jnp.exp2(
                value * (HD ** (-0.5) * LOG2E)
            ).astype(jnp.bfloat16)
    mixed = jnp.dot(prob[pl.ds(0, rows), :], v[...], preferred_element_type=jnp.float32)
    write(start, rows, (mixed[:, :HD] / mixed[:, HD:]).astype(jnp.bfloat16))


def group_kernel(
    first, heads, which, pair, apart, rows_from, xt_far, xi_far, w, w_own,
    gain, aq, bq, ak, bk, mask, *rest
):
    samples = len(which)
    steps = heads // pair
    items = samples * pair
    count = samples * 2 if apart else samples
    outs = rest[:count]
    xt, xi, buffers, q_s, k_s, v_s, flat_t, flat_i, scores, probs, tops, sems = rest[count:]
    tables = (aq, bq, ak, bk)
    slots = min(steps, 2)
    width = pair * 3 * HD

    def fetch(h, slot, stream):
        begin = pl.multiple_of((h * 2 + stream) * width, width)
        target = buffers.at[slot, stream]
        if rows_from is None:
            return [
                pltpu.make_async_copy(
                    w.at[:, pl.ds(begin, width)], target, sems.at[2 + slot * 2 + stream]
                )
            ]
        count = rows_from.shape[0]
        copies = []
        for n in range(count):
            if n == 0:
                begin_own = pl.multiple_of(
                    ((first // pair + h) * 2 + stream) * width, width
                )
                part = w_own.at[:, :, :, pl.ds(begin_own, width)]
            else:
                part = w.at[:, :, n - 1, :, pl.ds(begin, width)]
            copies.append(
                pltpu.make_async_copy(
                    part,
                    target.at[:, rows_from[n, 0], :, rows_from[n, 1], :, :],
                    sems.at[2 + (slot * 2 + stream) * count + n],
                )
            )
        return copies

    def start(copies):
        for copy in copies:
            copy.start()

    def wait(copies):
        for copy in copies:
            copy.wait()

    tokens = [
        pltpu.make_async_copy(far.at[pl.ds(which[0] * rows, samples * rows)], near, sems.at[n])
        for n, (far, near, rows) in enumerate(((xt_far, xt, TXT), (xi_far, xi, IMG)))
    ]
    start(fetch(0, 0, 0))
    tokens[0].start()
    lead = lax.broadcasted_iota(jnp.int32, (KEYS, HD), 1) == 0
    for slot in range(slots):
        for i in range(items):
            q_s[slot, i, :, HD:] = jnp.where(lead, 1.0, 0.0).astype(jnp.bfloat16)
            k_s[slot, i, :, HD:] = mask[which[i // pair]]
            k_s[slot, i, TOTAL:, :HD] = jnp.zeros((KEYS - TOTAL, HD), jnp.bfloat16)
            v_s[slot, i, :, HD:] = jnp.ones((KEYS, HD), jnp.bfloat16)
            v_s[slot, i, TOTAL:, :HD] = jnp.zeros((KEYS - TOTAL, HD), jnp.bfloat16)

    def project(h, stream):
        slot = h % 2
        project_stream(
            (xt, xi)[stream],
            buffers[slot, stream].reshape(D, width),
            0 if stream == 0 else TXT,
            samples,
            pair,
            gain,
            tables,
            q_s.at[slot],
            k_s.at[slot],
            v_s.at[slot],
            (flat_t, flat_i)[stream],
        )

    def attend(h, i):
        slot = h % 2

        def write(start, rows, block):
            column = (h * pair + i % pair) * HD
            column = column if isinstance(h, int) else pl.multiple_of(column, HD)
            if apart:
                begin = 0 if start < TXT else TXT // 2
                for k in range(2):
                    half = block[k * rows // 2 : (k + 1) * rows // 2]
                    outs[2 * (i // pair) + k][pl.ds(begin, rows // 2), pl.ds(column, HD)] = half
            else:
                outs[i // pair][pl.ds(start, rows), pl.ds(column, HD)] = block

        for n, (start, rows) in enumerate(((0, TXT), (TXT, IMG))):
            attend_block(
                q_s.at[slot, i],
                k_s.at[slot, i],
                v_s.at[slot, i],
                start,
                rows,
                write,
                scores.at[n],
                probs.at[n],
                tops.at[n],
            )

    wait(fetch(0, 0, 0))
    tokens[0].wait()
    start(fetch(0, 0, 1))
    tokens[1].start()
    project(0, 0)
    wait(fetch(0, 0, 1))
    tokens[1].wait()
    if steps > 1:
        for stream in range(2):
            start(fetch(1, 1, stream))
    project(0, 1)

    def step(h, carry):
        for stream in range(2):
            wait(fetch(h, h % 2, stream))

        @pl.when(h + 1 < steps)
        def _():
            for stream in range(2):
                start(fetch(h + 1, (h + 1) % 2, stream))

        half = max(items // 2, 1)
        project(h, 0)
        for i in range(half):
            attend(h - 1, i)
        project(h, 1)
        for i in range(half, items):
            attend(h - 1, i)
        return carry

    if steps > 1:
        lax.fori_loop(1, steps, step, 0)
    for i in range(items):
        attend(steps - 1, i)


def attend_group(xt, xi, gathered, own, rows_from, tables, mask, first, heads, which, pair, apart):
    samples = len(which)
    count = samples * 2 if apart else samples
    rows = TOTAL // 2 if apart else TOTAL
    slots = min(heads // pair, 2)
    in_vmem = pl.BlockSpec(memory_space=pltpu.VMEM)
    in_hbm = pl.BlockSpec(memory_space=pltpu.HBM)
    kernel = functools.partial(group_kernel, first, heads, which, pair, apart)
    if own is None:
        weight_args, weight_specs, buffer, quarters = [gathered], [in_hbm], (D,), 1
        body = lambda xt, xi, w, *rest: kernel(None, xt, xi, w, None, *rest)
    else:
        outers, cores, _, weight_rows, _ = gathered.shape
        quarters = rows_from.shape[0]
        ranks = quarters // 2
        weight_args = [gathered, own, rows_from]
        weight_specs = [in_hbm, in_hbm, pl.BlockSpec(memory_space=pltpu.SMEM)]
        buffer = (outers, 2, cores, ranks, weight_rows)
        body = lambda xt, xi, w, w_own, places, *rest: kernel(places, xt, xi, w, w_own, *rest)
    return pl.pallas_call(
        body,
        in_specs=[in_hbm] * 2 + weight_specs + [in_vmem] * (len(tables) + 1),
        out_specs=[in_vmem] * count,
        out_shape=[jax.ShapeDtypeStruct((rows, heads * HD), jnp.bfloat16)] * count,
        scratch_shapes=[
            pltpu.VMEM((samples * TXT, D), jnp.bfloat16),
            pltpu.VMEM((samples * IMG, D), jnp.bfloat16),
            pltpu.VMEM((slots, 2) + buffer + (pair * 3 * HD,), jnp.bfloat16),
        ]
        + [pltpu.VMEM((slots, samples * pair, KEYS, 2 * HD), jnp.bfloat16)] * 3
        + [
            pltpu.VMEM((samples * TXT, pair * 3 * HD), jnp.float32),
            pltpu.VMEM((samples * IMG, pair * 3 * HD), jnp.float32),
            pltpu.VMEM((2, IMG, KEYS), jnp.float32),
            pltpu.VMEM((2, IMG, KEYS), jnp.bfloat16),
            pltpu.VMEM((2, IMG, HD), jnp.float32),
            pltpu.SemaphoreType.DMA((2 + 2 * slots * quarters,)),
        ],
        compiler_params=pltpu.CompilerParams(vmem_limit_bytes=56 * 1024 * 1024),
        cost_estimate=pl.CostEstimate(
            flops=samples * heads * (2 * TOTAL * D * 3 * HD + 8 * TOTAL * TOTAL * HD),
            bytes_accessed=heads * D * 6 * HD * 2 + 2 * samples * TOTAL * D,
            transcendentals=samples * heads * TOTAL * TOTAL,
        ),
    )(xt, xi, *weight_args, *tables, mask)


def on_device(text_tokens, image_tokens, weights, qk_gain, mod_table, text_lengths, time_index):
    ranks = lax.axis_size("seq")
    reps = lax.axis_size("rep")
    split = 2 if (HEADS // ranks) % 2 == 0 and reps % 4 == 0 else 1
    cores = 2
    outers = reps // (split * cores)
    rank = lax.axis_index("seq")
    rep = lax.axis_index("rep")
    core = lax.rem(rep, cores)
    f_here = lax.rem(rep // cores, split)
    heads_here = HEADS // (split * ranks)
    cols = heads_here * HD
    weight_rows = weights.shape[1]
    text_rows = text_tokens.shape[1]
    image_rows = image_tokens.shape[1]
    weights = weights.transpose(0, 2, 1, 3)

    def permute(value, target):
        pairs = []
        for o in range(outers):
            for f in range(split):
                for c in range(cores):
                    for r in range(ranks):
                        tf, tc, tr = target(f, c, r)
                        pairs.append(
                            (
                                ((o * split + f) * cores + c) * ranks + r,
                                ((o * split + tf) * cores + tc) * ranks + tr % ranks,
                            )
                        )
        return lax.ppermute(value, ("rep", "seq"), pairs)

    def shift(value, flip, k):
        if flip == 0 and k % ranks == 0:
            return value
        return permute(value, lambda f, c, r: (f ^ flip, c, r + k))

    def source(k):
        return lax.rem(rank - k + ranks, ranks)

    def head_owner(flip, k):
        f = f_here ^ flip if split > 1 else 0
        return f * ranks + lax.rem(rank + k, ranks)

    groups = []
    first = 0
    for heads in head_groups(heads_here):
        groups.append((first, heads))
        first += heads
    pair = 2 if all(first % 2 == 0 and heads % 2 == 0 for first, heads in groups) else 1
    hops = [(a, k) for a in range(split) for k in range(ranks)]
    targets = jnp.stack([head_owner(a, k) * cols for a, k in hops]).astype(jnp.int32)
    places = jnp.stack([source(k) for _, k in hops]).astype(jnp.int32)
    rows_from = None
    if split > 1:
        rows_from = jnp.stack(
            [jnp.stack([f_here ^ a, source(k)]) for a, k in hops]
        ).astype(jnp.int32)
        own_columns = cut_pieces(weights, targets[:1], [(0, heads_here)], pair)[0][0]
        targets, own_columns = lax.optimization_barrier((targets[1:], own_columns))
        hops = hops[1:]
        places = jnp.arange(len(hops), dtype=jnp.int32)
    blocks = []
    for pieces in cut_pieces(weights, targets, groups, pair):
        pieces = [shift(piece, a, k) for piece, (a, k) in zip(pieces, hops)]
        block = stack_pieces(pieces, places)
        blocks.append(block.reshape(len(hops) * weight_rows, block.shape[-1]))

    gather_groups = [
        [(o * split + f) * cores + c for o in range(outers) for c in range(cores)]
        for f in range(split)
    ]

    def gather(block):
        return lax.all_gather(
            block,
            "rep",
            axis=0,
            tiled=True,
            axis_index_groups=gather_groups if split > 1 else None,
        )

    own_weight = gather(own_columns) if split > 1 else None
    modded = layer_modulate(time_index, mod_table, text_tokens[0], image_tokens[0])
    modded, blocks = lax.optimization_barrier((modded, blocks))
    own = [[shift(m, 0, k) for k in range(ranks)] for m in modded]
    other_image = shift(modded[1], 1, 0) if split > 1 else modded[1]
    texts, images = own
    if split > 1:
        texts = texts + [shift(piece, 1, 0) for piece in own[0]]
        images = images + [shift(other_image, 0, k) for k in range(ranks)]
    texts, images = [jnp.concatenate(pieces, axis=0) for pieces in (texts, images)]

    apart = ranks == 2
    order = [source(k) for k in range(ranks)]
    cosine_np, sine_np = rope_image_tables()

    def reorder(table):
        table = jnp.asarray(table)
        return jnp.concatenate(
            [lax.dynamic_slice_in_dim(table, r * image_rows, image_rows, 0) for r in order], axis=0
        )

    cosine, sine = reorder(cosine_np), reorder(sine_np)
    swapped = qk_gain.reshape(2, 2, HD // 2, 2)[..., ::-1].reshape(2, 2, HD)
    tables = [qk_gain[0]]
    for part in range(2):
        tables += [cosine * qk_gain[1, part], sine * swapped[1, part]]
    within = jnp.arange(text_rows, dtype=jnp.int32)
    masks = []
    for flip in range(split):
        live = shift(text_lengths, flip, 0)[0]
        column = [
            jnp.where(r * text_rows + within < live, 0.0, ABSENT).astype(jnp.float32)
            for r in order
        ]
        column.append(jnp.zeros((IMG,), jnp.float32))
        column.append(jnp.full((KEYS - TOTAL,), ABSENT, jnp.float32))
        masks.append(jnp.concatenate(column))
    mask = jnp.where(jnp.arange(HD) == 0, jnp.stack(masks)[:, :, None], 0.0).astype(jnp.bfloat16)

    blocks[-1], texts, images, tables, mask = lax.optimization_barrier(
        (blocks[-1], texts, images, tables, mask)
    )

    def attend(weight, first, heads):
        if split > 1:
            weight = weight.reshape(outers, cores, len(hops), weight_rows, weight.shape[-1])
        received, columns = [], []
        flips = list(range(split))
        calls = [flips] if heads <= pair else [[flip] for flip in reversed(flips)]
        for which in calls:
            parts = attend_group(
                texts, images, weight, own_quarter, rows_from, tables, mask,
                first, heads, tuple(which), pair, apart,
            )
            weight, parts = lax.optimization_barrier((weight, parts))
            if not apart:
                whole = parts
                parts = []
                for part in whole:
                    for k in range(ranks):
                        text = part[k * text_rows : (k + 1) * text_rows]
                        image = part[TXT + k * image_rows : TXT + (k + 1) * image_rows]
                        parts.append(jnp.concatenate([text, image], axis=0))
            for n, flip in enumerate(which):
                for k in range(ranks):
                    received.append(shift(parts[n * ranks + k], flip, ranks - k))
                    columns.append(head_owner(flip, k) * cols + first * HD)
        return received, columns

    def place(received, columns, outs):
        columns = jnp.stack(columns).astype(jnp.int32)
        return place_pieces(received, columns, outs, text_rows, image_rows)

    outs = []
    if split > 1:
        blocks[0], own_weight = lax.optimization_barrier((blocks[0], own_weight))
    weight = gather(blocks[0])
    own_quarter = None
    if split > 1:
        own_quarter = own_weight.reshape(outers, cores, weight_rows, own_weight.shape[-1])
    for g, (first, heads) in enumerate(groups):
        if g + 1 < len(groups):
            block, weight = lax.optimization_barrier((blocks[g + 1], weight))
            following = gather(block)
        outs = place(*attend(weight, first, heads), outs)
        weight = following
    return (outs[0][None], outs[1][None])


def solution(mesh):
    placed = (
        P("rep", "seq", None),
        P("rep", "seq", None),
        P(None, ("rep", "seq"), None, None),
        P(),
        P(),
        P("rep"),
        P("rep"),
    )
    return jax.shard_map(
        on_device,
        mesh=mesh,
        in_specs=placed,
        out_specs=(P("rep", "seq", None), P("rep", "seq", None)),
        check_vma=False,
    )
```
